256 devices in a mesh: dp: 256 (over x, y, z, core).
Axes of the slice: x: 4, y: 4, z: 8, core: 2. Of those that a mesh axis runs over, the one named last changes fastest.
Arguments:
- queries: bfloat16 [65536, 3584], P('dp'), may hold values from -2 to 2, as said below
- documents: bfloat16 [65536, 3584], P('dp'), may hold values from -2 to 2, as said below
Outputs:
- log_norm: float32 [65536], P('dp')
- query_grad: float32 [65536, 3584], P('dp')
- document_grad: float32 [65536, 3584], P('dp')
The draws below stay inside these ranges and needn't reach their ends.
Inputs may be any that keep to these rules, and one draw needn't show every extreme that they name: Real-valued embeddings; row i of documents is the positive of row i of queries. `documents`: Real-valued embeddings.
All inputs are finite; a program needn't handle non-finite values.
Results may differ from the reference program's by a relative error of at most 0.0025.
Values may be sent and summed in bfloat16 or wider, within the bound.
A program may use at most 128 MiB of HBM per device.

```python
import math
import jax
import jax.numpy as jnp
from jax import lax

D = 3584
ROWS = 256
BATCH = 65536


def query_values(key, lowest, highest, pinned):
    parts = jax.random.split(key, 2)
    base = jnp.clip(jax.random.normal(parts[0], (BATCH, D), jnp.float32), -4.0, 4.0)
    spread = jnp.exp(jax.random.uniform(parts[1], (BATCH, 1), jnp.float32, math.log(lowest), math.log(highest)))
    marked = jnp.arange(BATCH)[:, None] % 64 == 0
    spread = jnp.where(marked, jnp.float32(pinned), spread)
    return base * spread / math.sqrt(D)


def draw_queries(key, part):
    values = query_values(key, 0.8, 1.25, 1.25)
    return values.astype(jnp.bfloat16)


def draw_documents(key, part):
    values = query_values(key, 0.8, 1.25, 1.25)
    key = jax.random.fold_in(key, 11)
    noise = jax.random.normal(key, (BATCH, D), jnp.float32) / math.sqrt(D)
    result = 0.06 * values + noise
    return result.astype(jnp.bfloat16)


def setup_inputs(seed: int = 0) -> dict:
    arg_keys = jax.random.split(jax.random.key(seed), 3)
    return {
        "queries": draw_queries(jax.random.fold_in(arg_keys[2], 71), 0),
        "documents": draw_documents(jax.random.fold_in(arg_keys[2], 71), 0),
    }


def neighbours(stacked, index, blocks):
    pieces = [lax.dynamic_index_in_dim(stacked, ((index + offset + blocks) % blocks).astype(jnp.int32), 0, keepdims=False) for offset in range(-2, 3)]
    return jnp.concatenate(pieces, axis=0)


def block_tiles(query_blocks, document_blocks, index, blocks):
    own_q = lax.dynamic_index_in_dim(query_blocks, index.astype(jnp.int32), 0, keepdims=False)
    own_d = lax.dynamic_index_in_dim(document_blocks, index.astype(jnp.int32), 0, keepdims=False)
    near_q = neighbours(query_blocks, index, blocks)
    near_d = neighbours(document_blocks, index, blocks)
    score_qd = 100.0 * jnp.dot(own_q, near_d.T, preferred_element_type=jnp.float32)
    score_qq = 100.0 * jnp.dot(own_q, near_q.T, preferred_element_type=jnp.float32)
    score_dq = 100.0 * jnp.dot(own_d, near_q.T, preferred_element_type=jnp.float32)
    score_dd = 100.0 * jnp.dot(own_d, near_d.T, preferred_element_type=jnp.float32)
    return near_q, near_d, score_qd, score_qq, score_dq, score_dd


def reference(queries, documents):
    blocks = BATCH // ROWS
    query_blocks = queries.reshape(blocks, ROWS, D)
    document_blocks = documents.reshape(blocks, ROWS, D)
    self_mask = jnp.arange(5 * ROWS)[None, :] == (jnp.arange(ROWS)[:, None] + 2 * ROWS)
    minus_inf = jnp.float32(-jnp.inf)

    def forward(index):
        near_q, near_d, score_qd, score_qq, score_dq, score_dd = block_tiles(query_blocks, document_blocks, index, blocks)
        joined = jnp.concatenate([score_qd, jnp.where(self_mask, minus_inf, score_qq), jnp.where(self_mask, minus_inf, score_dq), jnp.where(self_mask, minus_inf, score_dd)], axis=1)
        highest = jnp.max(joined, axis=1)
        return highest + jnp.log(jnp.sum(jnp.exp(joined - highest[:, None]), axis=1))

    indices = jnp.arange(blocks, dtype=jnp.int32)
    norm_blocks = lax.map(forward, indices)

    def backward(index):
        near_q, near_d, score_qd, score_qq, score_dq, score_dd = block_tiles(query_blocks, document_blocks, index, blocks)
        own_norm = lax.dynamic_index_in_dim(norm_blocks, index.astype(jnp.int32), 0, keepdims=False)[:, None]
        near_norm = neighbours(norm_blocks, index, blocks)[None, :]
        diagonal = self_mask.astype(jnp.float32)
        zero = jnp.float32(0.0)
        weight_qd = jnp.exp(score_qd - own_norm) + jnp.where(self_mask, zero, jnp.exp(score_qd - near_norm)) - diagonal
        weight_qq = jnp.where(self_mask, zero, jnp.exp(score_qq - own_norm) + jnp.exp(score_qq - near_norm))
        weight_dq = jnp.exp(score_dq - near_norm) + jnp.where(self_mask, zero, jnp.exp(score_dq - own_norm)) - diagonal
        weight_dd = jnp.where(self_mask, zero, jnp.exp(score_dd - own_norm) + jnp.exp(score_dd - near_norm))
        grad_q = jnp.dot(weight_qd.astype(jnp.bfloat16), near_d, preferred_element_type=jnp.float32) + jnp.dot(weight_qq.astype(jnp.bfloat16), near_q, preferred_element_type=jnp.float32)
        grad_d = jnp.dot(weight_dq.astype(jnp.bfloat16), near_q, preferred_element_type=jnp.float32) + jnp.dot(weight_dd.astype(jnp.bfloat16), near_d, preferred_element_type=jnp.float32)
        return 100.0 * grad_q, 100.0 * grad_d

    grad_q, grad_d = lax.map(backward, indices)
    return norm_blocks.reshape(BATCH), grad_q.reshape(BATCH, D), grad_d.reshape(BATCH, D)
```

```python
import functools

import jax
import jax.numpy as jnp
from jax import lax
from jax.experimental import pallas as pl
from jax.experimental.pallas import tpu as pltpu
from jax.sharding import PartitionSpec as P

MESH = pl.DeviceIdType.MESH
SCALE = 100.0
WIDTH = 512
STRIP = 64


def lse(*terms):
    highest = functools.reduce(jnp.maximum, terms)
    return highest + jnp.log(sum(jnp.exp(term - highest) for term in terms))


def as_column(row):
    return jnp.broadcast_to(row, (128, row.shape[1])).T[:, :1]


def as_row(column):
    return jnp.broadcast_to(column, (column.shape[0], 128)).T[:1, :]


def cross(left, right):
    return lax.dot_general(left, right, (((1,), (1,)), ((), ())), preferred_element_type=jnp.float32)


def kernel(
    count,
    q_ref,
    d_ref,
    norm_ref,
    lq_ref,
    ld_ref,
    came_ref,
    x,
    s,
    w,
    wt,
    going,
    stat,
    out_msg,
    in_msg,
    own_sem,
    near_send,
    near_recv,
    far_send,
    far_recv,
    pass_send,
    pass_recv,
    grad_send,
    grad_recv,
    msg_send,
    msg_recv,
):
    rows, depth = q_ref.shape
    both = 2 * rows
    chunks = depth // WIDTH
    strips = both // STRIP
    me = lax.axis_index("dp")
    sign = 1 - 2 * lax.rem(me, 2)
    p = me + sign
    r = lax.rem(me - sign + count, count)
    f = lax.rem(me + 2 * sign + count, count)
    g = lax.rem(me - 2 * sign + count, count)

    def remote(src, dst, send, recv, to):
        return pltpu.make_async_remote_copy(
            src_ref=src, dst_ref=dst, send_sem=send, recv_sem=recv, device_id=(to,), device_id_type=MESH
        )

    def columns(k):
        return pl.ds(pl.multiple_of(k * WIDTH, WIDTH), WIDTH)

    def own_copy(half, k):
        ref = (q_ref, d_ref)[half]
        return pltpu.make_async_copy(
            ref.at[:, columns(k)], x.at[pl.ds(half * rows, rows), columns(k)], own_sem.at[half, k]
        )

    def near_copy(half, k):
        ref = (q_ref, d_ref)[half]
        return remote(
            ref.at[:, columns(k)],
            x.at[pl.ds(both + half * rows, rows), columns(k)],
            near_send.at[half, k],
            near_recv.at[half, k],
            p,
        )

    def far_copy(half, k):
        ref = (q_ref, d_ref)[half]
        return remote(
            ref.at[:, columns(k)],
            x.at[pl.ds(2 * both + half * rows, rows), columns(k)],
            far_send.at[half, k],
            far_recv.at[half, k],
            r,
        )

    def pass_copy(k):
        return remote(
            x.at[pl.ds(2 * both, both), columns(k)],
            x.at[pl.ds(3 * both, both), columns(k)],
            pass_send.at[k],
            pass_recv.at[k],
            p,
        )

    def grad_copy(k):
        return remote(
            going.at[:, columns(k)], came_ref.at[:, columns(k)], grad_send.at[k], grad_recv.at[k], f
        )

    def message(which, to):
        return remote(out_msg.at[which], in_msg.at[which], msg_send.at[which], msg_recv.at[which], to)

    def add_scores(block, k):
        at = pl.ds(block * both, both)
        s[at, :] += cross(x[at, columns(k)], x[0:both, columns(k)])

    def strip(block, c):
        return SCALE * s[pl.ds(pl.multiple_of(block * both + c * STRIP, STRIP), STRIP), :]

    def own_index(c):
        row = lax.broadcasted_iota(jnp.int32, (STRIP, both), 0) + c * STRIP
        col = lax.broadcasted_iota(jnp.int32, (STRIP, both), 1)
        return row, col

    def column_lse(block, mask=None):
        def values(c):
            tile = strip(block, c)
            if mask is not None:
                tile = jnp.where(mask(c), -jnp.inf, tile)
            return tile

        def highest(c, so_far):
            return jnp.maximum(so_far, jnp.max(values(c), axis=0, keepdims=True))

        top = lax.fori_loop(0, strips, highest, jnp.full((1, both), -jnp.inf, jnp.float32))

        def total(c, so_far):
            return so_far + jnp.sum(jnp.exp(values(c) - top), axis=0, keepdims=True)

        return top + jnp.log(lax.fori_loop(0, strips, total, jnp.zeros((1, both), jnp.float32)))

    def row_lse(block):
        def body(c, _):
            tile = strip(block, c)
            top = jnp.max(tile, axis=1, keepdims=True)
            value = top + jnp.log(jnp.sum(jnp.exp(tile - top), axis=1, keepdims=True))
            stat[pl.ds(pl.multiple_of(c * STRIP, STRIP), STRIP), :] = jnp.broadcast_to(value, (STRIP, 128))
            return 0

        lax.fori_loop(0, strips, body, 0)
        return lse(stat[0:rows, :1], stat[rows:both, :1])

    def merged(row):
        return lse(row[:, :rows], row[:, rows:])

    def post(which, row, to):
        out_msg[which] = jnp.broadcast_to(row, (8, rows))
        message(which, to).start()

    def weigh(block, column, row):
        stat[...] = jnp.broadcast_to(jnp.concatenate([column, column], axis=0), (both, 128))

        def body(c, _):
            tile = strip(block, c)
            theirs = stat[pl.ds(pl.multiple_of(c * STRIP, STRIP), STRIP), :1]
            value = jnp.exp(tile - theirs) + jnp.exp(tile - row)
            at = pl.multiple_of(block * both + c * STRIP, STRIP)
            w[pl.ds(at, STRIP), :] = value.astype(jnp.bfloat16)
            return 0

        lax.fori_loop(0, strips, body, 0)

    def turn(block):
        at = pl.ds(block * both, both)
        wt[:, at] = w[at, :].T

    def loop(body, low=0, high=chunks):
        def step(k, _):
            body(k)
            return 0

        lax.fori_loop(low, high, step, 0)

    s[...] = jnp.zeros_like(s)
    barrier = pltpu.get_barrier_semaphore()
    for device in (p, r, f, g):
        pl.semaphore_signal(barrier, inc=1, device_id=(device,), device_id_type=MESH)
    pl.semaphore_wait(barrier, 4)

    def send(k):
        for half in range(2):
            far_copy(half, k).start()
        for half in range(2):
            own_copy(half, k).start()
            near_copy(half, k).start()

    loop(send)

    def on_chip(k):
        for half in range(2):
            own_copy(half, k).wait()
            near_copy(half, k).wait_recv()
        add_scores(0, k)
        add_scores(1, k)

    loop(on_chip)

    def masked(c):
        row, col = own_index(c)
        same = lax.rem(row, rows) == lax.rem(col, rows)
        return same & ~((row >= rows) & (col < rows))

    chip_lse = lse(column_lse(0, masked), column_lse(1))

    def off_chip(k):
        for half in range(2):
            far_copy(half, k).wait_recv()
        pass_copy(k).start()
        add_scores(2, k)

        @pl.when(k > 0)
        def _():
            pass_copy(k - 1).wait_recv()
            add_scores(3, k - 1)

    loop(off_chip)
    far_lse = column_lse(2)
    pass_copy(chunks - 1).wait_recv()
    add_scores(3, chunks - 1)

    theirs = row_lse(3)
    post(0, as_row(theirs), f)
    local = merged(lse(chip_lse, far_lse, column_lse(3)))
    post(1, local, g)
    message(0, f).wait_recv()
    norm = lse(local, in_msg[0, :1, :])
    post(2, norm, p)
    post(3, norm, r)
    norm_ref[...] = jnp.broadcast_to(norm, (8, rows))
    norm_row = jnp.concatenate([norm, norm], axis=1)
    message(1, g).wait_recv()
    weigh(3, lse(as_column(in_msg[1, :1, :]), theirs), norm_row)

    def product(k):
        value = SCALE * jnp.dot(w[3 * both : 4 * both, :], x[0:both, columns(k)], preferred_element_type=jnp.float32)
        going[:, columns(k)] = value.astype(jnp.bfloat16)
        grad_copy(k).start()

    loop(product)

    stat[...] = jnp.broadcast_to(as_column(norm_row), (both, 128))

    def weigh_own(c, _):
        row, col = own_index(c)
        same = lax.rem(row, rows) == lax.rem(col, rows)
        tile = strip(0, c)
        across = jnp.exp(tile - norm_row)
        value = across + jnp.exp(tile - stat[pl.ds(pl.multiple_of(c * STRIP, STRIP), STRIP), :1])
        on_diagonal = jnp.where((row >= rows) == (col >= rows), 0.0, across - 1.0)
        value = jnp.where(same, on_diagonal, value)
        wt[pl.ds(pl.multiple_of(c * STRIP, STRIP), STRIP), 0:both] = value.astype(jnp.bfloat16)
        return 0

    lax.fori_loop(0, strips, weigh_own, 0)
    message(2, p).wait_recv()
    weigh(1, as_column(in_msg[2, :1, :]), norm_row)
    message(3, r).wait_recv()
    weigh(2, as_column(in_msg[3, :1, :]), norm_row)
    for block in (1, 2, 3):
        turn(block)

    def local_gradient(k):
        value = SCALE * jnp.dot(wt[...], x[:, columns(k)], preferred_element_type=jnp.float32)
        lq_ref[:, columns(k)] = value[:rows]
        ld_ref[:, columns(k)] = value[rows:]

    loop(local_gradient)

    def ends(k):
        for half in range(2):
            near_copy(half, k).wait_send()
            far_copy(half, k).wait_send()
        pass_copy(k).wait_send()
        grad_copy(k).wait_send()
        grad_copy(k).wait_recv()

    for which, to in enumerate((f, g, p, r)):
        message(which, to).wait_send()
    loop(ends)


def on_device(queries, documents, count):
    rows, depth = queries.shape
    both = 2 * rows
    chunks = depth // WIDTH
    dma = pltpu.SemaphoreType.DMA
    norm, part_q, part_d, came = pl.pallas_call(
        functools.partial(kernel, count),
        out_shape=(
            jax.ShapeDtypeStruct((8, rows), jnp.float32),
            pltpu.VMEM((rows, depth), jnp.float32),
            pltpu.VMEM((rows, depth), jnp.float32),
            pltpu.VMEM((both, depth), jnp.bfloat16),
        ),
        in_specs=[pl.BlockSpec(memory_space=pltpu.HBM)] * 2,
        out_specs=(pl.BlockSpec(memory_space=pltpu.VMEM),) * 4,
        scratch_shapes=[
            pltpu.VMEM((4 * both, depth), jnp.bfloat16),
            pltpu.VMEM((4 * both, both), jnp.float32),
            pltpu.VMEM((4 * both, both), jnp.bfloat16),
            pltpu.VMEM((both, 4 * both), jnp.bfloat16),
            pltpu.VMEM((both, depth), jnp.bfloat16),
            pltpu.VMEM((both, 128), jnp.float32),
            pltpu.VMEM((4, 8, rows), jnp.float32),
            pltpu.VMEM((4, 8, rows), jnp.float32),
            dma((2, chunks)),
            dma((2, chunks)),
            dma((2, chunks)),
            dma((2, chunks)),
            dma((2, chunks)),
            dma((chunks,)),
            dma((chunks,)),
            dma((chunks,)),
            dma((chunks,)),
            dma((4,)),
            dma((4,)),
        ],
        compiler_params=pltpu.CompilerParams(
            collective_id=0, has_side_effects=True, vmem_limit_bytes=44 << 20
        ),
    )(queries, documents)
    came = came.astype(jnp.float32)
    return norm[0], part_q + came[:rows], part_d + came[rows:]


def solution(mesh):
    return jax.shard_map(
        functools.partial(on_device, count=mesh.shape["dp"]),
        mesh=mesh,
        in_specs=(P("dp", None), P("dp", None)),
        out_specs=(P("dp"), P("dp", None), P("dp", None)),
        check_vma=False,
    )
```

```python
import functools

import jax
import jax.numpy as jnp
from jax import lax
from jax.experimental import pallas as pl
from jax.experimental.pallas import tpu as pltpu
from jax.sharding import PartitionSpec as P

MESH = pl.DeviceIdType.MESH
SCALE = 100.0
WIDTH = 512
GROUP = 128


def lse(*terms):
    highest = functools.reduce(jnp.maximum, terms)
    return highest + jnp.log(sum(jnp.exp(term - highest) for term in terms))


def as_column(row):
    return jnp.broadcast_to(row, (128, row.shape[1])).T[:, :1]


def as_row(column):
    return jnp.broadcast_to(column, (column.shape[0], 128)).T[:1, :]


def cross(left, right):
    return lax.dot_general(left, right, (((1,), (1,)), ((), ())), preferred_element_type=jnp.float32)


def kernel(
    count,
    q_ref,
    d_ref,
    norm_ref,
    lq_ref,
    ld_ref,
    x,
    s,
    w,
    wt,
    going,
    came,
    stat,
    out_msg,
    in_msg,
    own_sem,
    near_send,
    near_recv,
    far_send,
    far_recv,
    pass_send,
    pass_recv,
    grad_send,
    grad_recv,
    msg_send,
    msg_recv,
):
    rows, depth = q_ref.shape
    both = 2 * rows
    chunks = depth // WIDTH
    groups = both // GROUP
    me = lax.axis_index("dp")
    sign = 1 - 2 * lax.rem(me, 2)
    p = me + sign
    r = lax.rem(me - sign + count, count)
    f = lax.rem(me + 2 * sign + count, count)
    g = lax.rem(me - 2 * sign + count, count)

    def remote(src, dst, send, recv, to):
        return pltpu.make_async_remote_copy(
            src_ref=src, dst_ref=dst, send_sem=send, recv_sem=recv, device_id=(to,), device_id_type=MESH
        )

    def columns(k):
        return pl.ds(pl.multiple_of(k * WIDTH, WIDTH), WIDTH)

    def part(block, group):
        return pl.ds(block * both + group * GROUP, GROUP)

    def source(group):
        half, first = divmod(group * GROUP, rows)
        return (q_ref, d_ref)[half].at[pl.ds(first, GROUP), :]

    def own_copy(half, k):
        ref = (q_ref, d_ref)[half]
        return pltpu.make_async_copy(
            ref.at[:, columns(k)], x.at[pl.ds(half * rows, rows), columns(k)], own_sem.at[half, k]
        )

    def near_copy(half, k):
        ref = (q_ref, d_ref)[half]
        return remote(
            ref.at[:, columns(k)],
            x.at[pl.ds(both + half * rows, rows), columns(k)],
            near_send.at[half, k],
            near_recv.at[half, k],
            p,
        )

    def far_copy(group, k):
        return remote(
            source(group).at[:, columns(k)],
            x.at[part(2, group), columns(k)],
            far_send.at[group, k],
            far_recv.at[group, k],
            r,
        )

    def pass_copy(group, k):
        return remote(
            x.at[part(2, group), columns(k)],
            x.at[part(3, group), columns(k)],
            pass_send.at[group, k],
            pass_recv.at[group, k],
            p,
        )

    def grad_copy(group, k):
        at = (pl.ds(group * GROUP, GROUP), columns(k))
        return remote(going.at[at], came.at[at], grad_send.at[group, k], grad_recv.at[group, k], f)

    def message(which, to):
        return remote(out_msg.at[which], in_msg.at[which], msg_send.at[which], msg_recv.at[which], to)

    def add_scores(at, k):
        s[at, :] += cross(x[at, columns(k)], x[0:both, columns(k)])

    def tile(block, group):
        return SCALE * s[part(block, group), :]

    def same_pair(group):
        row = lax.broadcasted_iota(jnp.int32, (GROUP, both), 0) + group * GROUP
        col = lax.broadcasted_iota(jnp.int32, (GROUP, both), 1)
        return (row == col) | (row == col + rows) | (row + rows == col), col < rows

    def column_lse(value):
        top = jnp.max(value, axis=0, keepdims=True)
        return top + jnp.log(jnp.sum(jnp.exp(value - top), axis=0, keepdims=True))

    def row_lse(value):
        top = jnp.max(value, axis=1, keepdims=True)
        return top + jnp.log(jnp.sum(jnp.exp(value - top), axis=1, keepdims=True))

    def post(which, row, to):
        out_msg[which] = jnp.broadcast_to(row, (8, rows))
        message(which, to).start()

    def weigh(block, group, column, row):
        first = group * GROUP % rows
        value = tile(block, group)
        value = jnp.exp(value - column[first : first + GROUP]) + jnp.exp(value - row)
        w[part(block, group), :] = value.astype(jnp.bfloat16)

    def turn(block):
        at = pl.ds(block * both, both)
        wt[:, at] = w[at, :].T

    def loop(body):
        def step(k, _):
            body(k)
            return 0

        lax.fori_loop(0, chunks, step, 0)

    barrier = pltpu.get_barrier_semaphore()
    for device in (p, r, f, g):
        pl.semaphore_signal(barrier, inc=1, device_id=(device,), device_id_type=MESH)
    s[...] = jnp.zeros_like(s)
    pl.semaphore_wait(barrier, 4)

    def send_first(k):
        far_copy(0, k).start()
        for half in range(2):
            own_copy(half, k).start()
            near_copy(half, k).start()

    loop(send_first)
    for group in range(1, groups):
        loop(lambda k: far_copy(group, k).start())

    def on_chip(k):
        for half in range(2):
            own_copy(half, k).wait()
            near_copy(half, k).wait_recv()
        add_scores(pl.ds(0, 2 * both), k)

    loop(on_chip)
    held = []
    for group in range(groups):
        same, query = same_pair(group)
        keep = query if group * GROUP >= rows else False
        held.append(column_lse(jnp.where(same & ~keep, -jnp.inf, tile(0, group))))
        held.append(column_lse(tile(1, group)))
    chip_lse = lse(*held)

    for group in range(groups):

        def off_chip(k):
            far_copy(group, k).wait_recv()
            pass_copy(group, k).start()
            add_scores(part(2, group), k)

            @pl.when(k > 0)
            def _():
                pass_copy(group, k - 1).wait_recv()
                add_scores(part(3, group), k - 1)

        loop(off_chip)
        chip_lse = lse(chip_lse, column_lse(tile(2, group)))
        pass_copy(group, chunks - 1).wait_recv()
        add_scores(part(3, group), chunks - 1)
        value = tile(3, group)
        stat[pl.ds(group * GROUP, GROUP), :] = jnp.broadcast_to(row_lse(value), (GROUP, 128))
        if group < groups - 1:
            chip_lse = lse(chip_lse, column_lse(value))

    theirs = as_row(lse(stat[0:rows, :], stat[rows:both, :]))
    post(0, theirs, f)
    chip_lse = lse(chip_lse, column_lse(value))
    local = lse(chip_lse[:, :rows], chip_lse[:, rows:])
    post(1, local, g)
    message(0, f).wait_recv()
    norm = lse(local, in_msg[0, :1, :])
    norm_row = jnp.concatenate([norm, norm], axis=1)
    message(1, g).wait_recv()
    far_column = as_column(lse(in_msg[1, :1, :], theirs))

    for group in range(groups):
        weigh(3, group, far_column, norm_row)

        def product(k):
            value = jnp.dot(w[part(3, group), :], x[0:both, columns(k)], preferred_element_type=jnp.float32)
            going[pl.ds(group * GROUP, GROUP), columns(k)] = (SCALE * value).astype(jnp.bfloat16)
            grad_copy(group, k).start()

        loop(product)
        if group == 0:
            post(2, norm, p)
            post(3, norm, r)
            norm_ref[...] = norm

    own_column = as_column(norm)
    for group in range(groups):
        same, query = same_pair(group)
        if group * GROUP >= rows:
            query = ~query
        first = group * GROUP % rows
        value = tile(0, group)
        across = jnp.exp(value - norm_row)
        value = across + jnp.exp(value - own_column[first : first + GROUP])
        value = jnp.where(same, jnp.where(query, 0.0, across - 1.0), value)
        wt[pl.ds(group * GROUP, GROUP), 0:both] = value.astype(jnp.bfloat16)
    for block, which, to in ((1, 2, p), (2, 3, r)):
        message(which, to).wait_recv()
        column = as_column(in_msg[which, :1, :])
        for group in range(groups):
            weigh(block, group, column, norm_row)
    for block in (1, 2, 3):
        turn(block)

    def local_gradient(k):
        value = SCALE * jnp.dot(wt[...], x[:, columns(k)], preferred_element_type=jnp.float32)
        lq_ref[:, columns(k)] = value[:rows]
        ld_ref[:, columns(k)] = value[rows:]

    loop(local_gradient)

    def sent(k):
        for half in range(2):
            near_copy(half, k).wait_send()
        for group in range(groups):
            far_copy(group, k).wait_send()
            pass_copy(group, k).wait_send()

    loop(sent)
    for which, to in enumerate((f, g, p, r)):
        message(which, to).wait_send()
    for group in range(groups):
        half, first = divmod(group * GROUP, rows)
        out = (lq_ref, ld_ref)[half]

        def add_terms(k):
            grad_copy(group, k).wait_recv()
            terms = came[pl.ds(group * GROUP, GROUP), columns(k)]
            out[pl.ds(first, GROUP), columns(k)] += terms.astype(jnp.float32)
            grad_copy(group, k).wait_send()

        loop(add_terms)


def on_device(queries, documents, count):
    rows, depth = queries.shape
    both = 2 * rows
    chunks = depth // WIDTH
    groups = both // GROUP
    dma = pltpu.SemaphoreType.DMA
    norm, grad_q, grad_d = pl.pallas_call(
        functools.partial(kernel, count),
        out_shape=(
            jax.ShapeDtypeStruct((1, rows), jnp.float32),
            pltpu.VMEM((rows, depth), jnp.float32),
            pltpu.VMEM((rows, depth), jnp.float32),
        ),
        in_specs=[pl.BlockSpec(memory_space=pltpu.HBM)] * 2,
        out_specs=(pl.BlockSpec(memory_space=pltpu.VMEM),) * 3,
        scratch_shapes=[
            pltpu.VMEM((4 * both, depth), jnp.bfloat16),
            pltpu.VMEM((4 * both, both), jnp.float32),
            pltpu.VMEM((4 * both, both), jnp.bfloat16),
            pltpu.VMEM((both, 4 * both), jnp.bfloat16),
            pltpu.VMEM((both, depth), jnp.bfloat16),
            pltpu.VMEM((both, depth), jnp.bfloat16),
            pltpu.VMEM((both, 128), jnp.float32),
            pltpu.VMEM((4, 8, rows), jnp.float32),
            pltpu.VMEM((4, 8, rows), jnp.float32),
            dma((2, chunks)),
            dma((2, chunks)),
            dma((2, chunks)),
            dma((groups, chunks)),
            dma((groups, chunks)),
            dma((groups, chunks)),
            dma((groups, chunks)),
            dma((groups, chunks)),
            dma((groups, chunks)),
            dma((4,)),
            dma((4,)),
        ],
        compiler_params=pltpu.CompilerParams(
            collective_id=0, has_side_effects=True, vmem_limit_bytes=56 << 20
        ),
    )(queries, documents)
    return norm.reshape(rows), grad_q, grad_d


def solution(mesh):
    return jax.shard_map(
        functools.partial(on_device, count=mesh.shape["dp"]),
        mesh=mesh,
        in_specs=(P("dp", None), P("dp", None)),
        out_specs=(P("dp"), P("dp", None), P("dp", None)),
        check_vma=False,
    )
```

```python
import functools

import jax
import jax.numpy as jnp
from jax import lax
from jax.experimental import pallas as pl
from jax.experimental.pallas import tpu as pltpu
from jax.sharding import PartitionSpec as P

MESH = pl.DeviceIdType.MESH
SCALE = 100.0
WIDTH = 512
GROUP = 128
PIECES = 4


def lse(*terms):
    highest = functools.reduce(jnp.maximum, terms)
    return highest + jnp.log(sum(jnp.exp(term - highest) for term in terms))


def as_column(row):
    return jnp.broadcast_to(row, (128, row.shape[1])).T[:, :1]


def as_row(column):
    return jnp.broadcast_to(column, (column.shape[0], 128)).T[:1, :]


def cross(left, right):
    return lax.dot_general(left, right, (((1,), (1,)), ((), ())), preferred_element_type=jnp.float32)


def kernel(
    count,
    q_ref,
    d_ref,
    norm_ref,
    lq_ref,
    ld_ref,
    x,
    s,
    w,
    wt,
    going,
    came,
    stat,
    out_msg,
    in_msg,
    own_sem,
    near_send,
    near_recv,
    far_send,
    far_recv,
    pass_send,
    pass_recv,
    grad_send,
    grad_recv,
    msg_send,
    msg_recv,
):
    rows, depth = q_ref.shape
    both = 2 * rows
    chunks = depth // WIDTH
    groups = both // GROUP
    me = lax.axis_index("dp")
    sign = 1 - 2 * lax.rem(me, 2)
    p = me + sign
    r = lax.rem(me - sign + count, count)
    f = lax.rem(me + 2 * sign + count, count)
    g = lax.rem(me - 2 * sign + count, count)

    def remote(src, dst, send, recv, to):
        return pltpu.make_async_remote_copy(
            src_ref=src, dst_ref=dst, send_sem=send, recv_sem=recv, device_id=(to,), device_id_type=MESH
        )

    def columns(k):
        return pl.ds(pl.multiple_of(k * WIDTH, WIDTH), WIDTH)

    def part(block, group):
        return pl.ds(block * both + group * GROUP, GROUP)

    def source(group):
        half, first = divmod(group * GROUP, rows)
        return (q_ref, d_ref)[half].at[pl.ds(first, GROUP), :]

    def own_copy(half, k):
        ref = (q_ref, d_ref)[half]
        return pltpu.make_async_copy(
            ref.at[:, columns(k)], x.at[pl.ds(half * rows, rows), columns(k)], own_sem.at[half, k]
        )

    def near_copy(half, k):
        ref = (q_ref, d_ref)[half]
        return remote(
            ref.at[:, columns(k)],
            x.at[pl.ds(both + half * rows, rows), columns(k)],
            near_send.at[half, k],
            near_recv.at[half, k],
            p,
        )

    def far_copy(group, k):
        return remote(
            source(group).at[:, columns(k)],
            x.at[part(2, group), columns(k)],
            far_send.at[group, k],
            far_recv.at[group, k],
            r,
        )

    def pass_copy(group, k):
        return remote(
            x.at[part(2, group), columns(k)],
            x.at[part(3, group), columns(k)],
            pass_send.at[group, k],
            pass_recv.at[group, k],
            p,
        )

    def direct_copy():
        return remote(
            source(groups - 1).at[:, columns(chunks - 1)],
            x.at[part(3, groups - 1), columns(chunks - 1)],
            pass_send.at[groups - 1, chunks - 1],
            pass_recv.at[groups - 1, chunks - 1],
            g,
        )

    def grad_copy(group, k):
        at = (pl.ds(group * GROUP, GROUP), columns(k))
        return remote(going.at[at], came.at[at], grad_send.at[group, k], grad_recv.at[group, k], f)

    def message(which, to):
        return remote(out_msg.at[which], in_msg.at[which], msg_send.at[which], msg_recv.at[which], to)

    def add_scores(at, k):
        s[at, :] += cross(x[at, columns(k)], x[0:both, columns(k)])

    def tile(block, group):
        return SCALE * s[part(block, group), :]

    def same_pair(group):
        row = lax.broadcasted_iota(jnp.int32, (GROUP, both), 0) + group * GROUP
        col = lax.broadcasted_iota(jnp.int32, (GROUP, both), 1)
        return (row == col) | (row == col + rows) | (row + rows == col), col < rows

    def column_lse(value):
        top = jnp.max(value, axis=0, keepdims=True)
        return top + jnp.log(jnp.sum(jnp.exp(value - top), axis=0, keepdims=True))

    def row_lse(value):
        top = jnp.max(value, axis=1, keepdims=True)
        return top + jnp.log(jnp.sum(jnp.exp(value - top), axis=1, keepdims=True))

    def post(which, row, to):
        out_msg[which] = jnp.broadcast_to(row, (8, rows))
        message(which, to).start()

    def weigh(block, group, column, row):
        first = group * GROUP % rows
        value = tile(block, group)
        value = jnp.exp(value - column[first : first + GROUP]) + jnp.exp(value - row)
        w[part(block, group), :] = value.astype(jnp.bfloat16)

    def turn(block):
        at = pl.ds(block * both, both)
        wt[:, at] = w[at, :].T

    def loop(body, steps=chunks):
        def step(k, _):
            body(k)
            return 0

        lax.fori_loop(0, steps, step, 0)

    barrier = pltpu.get_barrier_semaphore()
    for device in (p, r, f, g):
        pl.semaphore_signal(barrier, inc=1, device_id=(device,), device_id_type=MESH)
    s[...] = jnp.zeros_like(s)
    pl.semaphore_wait(barrier, 4)

    def send_first(k):
        far_copy(0, k).start()
        for half in range(2):
            own_copy(half, k).start()
            near_copy(half, k).start()

    loop(send_first)
    for group in range(1, groups - 1):
        loop(lambda k: far_copy(group, k).start())
    loop(lambda k: far_copy(groups - 1, k).start(), chunks - 1)
    direct_copy().start()
    far_copy(groups - 1, chunks - 1).start()

    def on_chip(k):
        for half in range(2):
            own_copy(half, k).wait()
            near_copy(half, k).wait_recv()
        add_scores(pl.ds(0, 2 * both), k)

    loop(on_chip)
    held = []
    for group in range(groups):
        same, query = same_pair(group)
        keep = query if group * GROUP >= rows else False
        held.append(column_lse(jnp.where(same & ~keep, -jnp.inf, tile(0, group))))
        held.append(column_lse(tile(1, group)))
    chip_lse = lse(*held)

    for group in range(groups):

        def off_chip(k):
            far_copy(group, k).wait_recv()
            pass_copy(group, k).start()
            add_scores(part(2, group), k)

            @pl.when(k > 0)
            def _():
                pass_copy(group, k - 1).wait_recv()
                add_scores(part(3, group), k - 1)

        last = group == groups - 1
        loop(off_chip, chunks - 1)
        if not last:
            far_copy(group, chunks - 1).wait_recv()
            pass_copy(group, chunks - 1).start()
            add_scores(part(2, group), chunks - 1)
        pass_copy(group, chunks - 2).wait_recv()
        add_scores(part(3, group), chunks - 2)
        pass_copy(group, chunks - 1).wait_recv()
        add_scores(part(3, group), chunks - 1)
        value = tile(3, group)
        stat[pl.ds(group * GROUP, GROUP), :] = jnp.broadcast_to(row_lse(value), (GROUP, 128))
        if last:
            theirs = as_row(lse(stat[0:rows, :], stat[rows:both, :]))
            post(0, theirs, f)
            chip_lse = lse(chip_lse, column_lse(value))
            far_copy(group, chunks - 1).wait_recv()
            add_scores(part(2, group), chunks - 1)
            chip_lse = lse(chip_lse, column_lse(tile(2, group)))
        else:
            chip_lse = lse(chip_lse, column_lse(value), column_lse(tile(2, group)))

    local = lse(chip_lse[:, :rows], chip_lse[:, rows:])
    post(1, local, g)
    message(0, f).wait_recv()
    norm = lse(local, in_msg[0, :1, :])
    norm_row = jnp.concatenate([norm, norm], axis=1)
    message(1, g).wait_recv()
    far_column = as_column(lse(in_msg[1, :1, :], theirs))

    for group in range(groups):
        weigh(3, group, far_column, norm_row)

        def product(k):
            value = jnp.dot(w[part(3, group), :], x[0:both, columns(k)], preferred_element_type=jnp.float32)
            going[pl.ds(group * GROUP, GROUP), columns(k)] = (SCALE * value).astype(jnp.bfloat16)
            grad_copy(group, k).start()

        loop(product)
        if group == 0:
            post(2, norm, p)
            post(3, norm, r)
            norm_ref[...] = norm

    own_column = as_column(norm)
    for group in range(groups):
        same, query = same_pair(group)
        if group * GROUP >= rows:
            query = ~query
        first = group * GROUP % rows
        value = tile(0, group)
        across = jnp.exp(value - norm_row)
        value = across + jnp.exp(value - own_column[first : first + GROUP])
        value = jnp.where(same, jnp.where(query, 0.0, across - 1.0), value)
        wt[pl.ds(group * GROUP, GROUP), 0:both] = value.astype(jnp.bfloat16)
    for block, which, to in ((1, 2, p), (2, 3, r)):
        message(which, to).wait_recv()
        column = as_column(in_msg[which, :1, :])
        for group in range(groups):
            weigh(block, group, column, norm_row)
    for block in (1, 2, 3):
        turn(block)

    def local_gradient(k):
        value = SCALE * jnp.dot(wt[...], x[:, columns(k)], preferred_element_type=jnp.float32)
        lq_ref[:, columns(k)] = value[:rows]
        ld_ref[:, columns(k)] = value[rows:]

    loop(local_gradient)

    def sent(k):
        for half in range(2):
            near_copy(half, k).wait_send()
        for group in range(groups):
            far_copy(group, k).wait_send()

    def passed(k):
        for group in range(groups - 1):
            pass_copy(group, k).wait_send()

    loop(sent)
    loop(passed)
    loop(lambda k: pass_copy(groups - 1, k).wait_send(), chunks - 1)
    direct_copy().wait_send()
    for which, to in enumerate((f, g, p, r)):
        message(which, to).wait_send()
    for group in range(groups):
        half, first = divmod(group * GROUP, rows)
        out = (lq_ref, ld_ref)[half]

        def add_terms(k):
            grad_copy(group, k).wait_recv()
            terms = came[pl.ds(group * GROUP, GROUP), columns(k)]
            out[pl.ds(first, GROUP), columns(k)] += terms.astype(jnp.float32)
            grad_copy(group, k).wait_send()

        loop(add_terms)


def write_out(norm_in, q_in, d_in, norm_out, q_out, d_out, sem):
    copies = []
    rows = q_in.shape[0] // PIECES
    for which, (source, target) in enumerate(((q_in, q_out), (d_in, d_out))):
        for piece in range(PIECES):
            at = pl.ds(piece * rows, rows)
            copies.append(pltpu.make_async_copy(source.at[at, :], target.at[at, :], sem.at[which, piece]))
    copies.append(pltpu.make_async_copy(norm_in, norm_out, sem.at[2, 0]))
    for copy in copies:
        copy.start()
    for copy in copies:
        copy.wait()


def on_device(queries, documents, count):
    rows, depth = queries.shape
    both = 2 * rows
    chunks = depth // WIDTH
    groups = both // GROUP
    dma = pltpu.SemaphoreType.DMA
    norm, grad_q, grad_d = pl.pallas_call(
        functools.partial(kernel, count),
        out_shape=(
            pltpu.VMEM((1, rows), jnp.float32),
            pltpu.VMEM((rows, depth), jnp.float32),
            pltpu.VMEM((rows, depth), jnp.float32),
        ),
        in_specs=[pl.BlockSpec(memory_space=pltpu.HBM)] * 2,
        out_specs=(pl.BlockSpec(memory_space=pltpu.VMEM),) * 3,
        scratch_shapes=[
            pltpu.VMEM((4 * both, depth), jnp.bfloat16),
            pltpu.VMEM((4 * both, both), jnp.float32),
            pltpu.VMEM((4 * both, both), jnp.bfloat16),
            pltpu.VMEM((both, 4 * both), jnp.bfloat16),
            pltpu.VMEM((both, depth), jnp.bfloat16),
            pltpu.VMEM((both, depth), jnp.bfloat16),
            pltpu.VMEM((both, 128), jnp.float32),
            pltpu.VMEM((4, 8, rows), jnp.float32),
            pltpu.VMEM((4, 8, rows), jnp.float32),
            dma((2, chunks)),
            dma((2, chunks)),
            dma((2, chunks)),
            dma((groups, chunks)),
            dma((groups, chunks)),
            dma((groups, chunks)),
            dma((groups, chunks)),
            dma((groups, chunks)),
            dma((groups, chunks)),
            dma((4,)),
            dma((4,)),
        ],
        compiler_params=pltpu.CompilerParams(
            collective_id=0, has_side_effects=True, vmem_limit_bytes=56 << 20
        ),
    )(queries, documents)
    norm, grad_q, grad_d = pl.pallas_call(
        write_out,
        out_shape=(
            jax.ShapeDtypeStruct((1, rows), jnp.float32),
            jax.ShapeDtypeStruct((rows, depth), jnp.float32),
            jax.ShapeDtypeStruct((rows, depth), jnp.float32),
        ),
        in_specs=[pl.BlockSpec(memory_space=pltpu.VMEM)] * 3,
        out_specs=(pl.BlockSpec(memory_space=pl.ANY),) * 3,
        scratch_shapes=[dma((3, PIECES))],
        compiler_params=pltpu.CompilerParams(vmem_limit_bytes=16 << 20),
    )(*[pltpu.with_memory_space_constraint(a, pltpu.VMEM) for a in (norm, grad_q, grad_d)])
    return norm.reshape(rows), grad_q, grad_d


def solution(mesh):
    return jax.shard_map(
        functools.partial(on_device, count=mesh.shape["dp"]),
        mesh=mesh,
        in_specs=(P("dp", None), P("dp", None)),
        out_specs=(P("dp"), P("dp", None), P("dp", None)),
        check_vma=False,
    )
```

```python
import functools

import jax
import jax.numpy as jnp
from jax import lax
from jax.experimental import pallas as pl
from jax.experimental.pallas import tpu as pltpu
from jax.sharding import PartitionSpec as P

MESH = pl.DeviceIdType.MESH
SCALE = 100.0
WIDTH = 512
GROUP = 128
PIECES = 8


def lse(*terms):
    highest = functools.reduce(jnp.maximum, terms)
    return highest + jnp.log(sum(jnp.exp(term - highest) for term in terms))


def as_column(row):
    return jnp.broadcast_to(row, (128, row.shape[1])).T[:, :1]


def as_row(column):
    return jnp.broadcast_to(column, (column.shape[0], 128)).T[:1, :]


def cross(left, right):
    return lax.dot_general(left, right, (((1,), (1,)), ((), ())), preferred_element_type=jnp.float32)


def kernel(
    count,
    q_ref,
    d_ref,
    norm_ref,
    lq_ref,
    ld_ref,
    x,
    s,
    w,
    wt,
    going,
    came,
    stat,
    out_msg,
    in_msg,
    own_sem,
    near_send,
    near_recv,
    far_send,
    far_recv,
    pass_send,
    pass_recv,
    grad_send,
    grad_recv,
    msg_send,
    msg_recv,
):
    rows, depth = q_ref.shape
    both = 2 * rows
    chunks = depth // WIDTH
    groups = both // GROUP
    me = lax.axis_index("dp")
    sign = 1 - 2 * lax.rem(me, 2)
    p = me + sign
    r = lax.rem(me - sign + count, count)
    f = lax.rem(me + 2 * sign + count, count)
    g = lax.rem(me - 2 * sign + count, count)

    def remote(src, dst, send, recv, to):
        return pltpu.make_async_remote_copy(
            src_ref=src, dst_ref=dst, send_sem=send, recv_sem=recv, device_id=(to,), device_id_type=MESH
        )

    def columns(k):
        return pl.ds(pl.multiple_of(k * WIDTH, WIDTH), WIDTH)

    def part(block, group):
        return pl.ds(block * both + group * GROUP, GROUP)

    def source(group):
        half, first = divmod(group * GROUP, rows)
        return (q_ref, d_ref)[half].at[pl.ds(first, GROUP), :]

    def own_copy(half, k):
        ref = (q_ref, d_ref)[half]
        return pltpu.make_async_copy(
            ref.at[:, columns(k)], x.at[pl.ds(half * rows, rows), columns(k)], own_sem.at[half, k]
        )

    def near_copy(half, k):
        ref = (q_ref, d_ref)[half]
        return remote(
            ref.at[:, columns(k)],
            x.at[pl.ds(both + half * rows, rows), columns(k)],
            near_send.at[half, k],
            near_recv.at[half, k],
            p,
        )

    def far_copy(group, k):
        return remote(
            source(group).at[:, columns(k)],
            x.at[part(2, group), columns(k)],
            far_send.at[group, k],
            far_recv.at[group, k],
            r,
        )

    def pass_copy(group, k):
        return remote(
            x.at[part(2, group), columns(k)],
            x.at[part(3, group), columns(k)],
            pass_send.at[group, k],
            pass_recv.at[group, k],
            p,
        )

    def direct_copy():
        return remote(
            source(groups - 1).at[:, columns(chunks - 1)],
            x.at[part(3, groups - 1), columns(chunks - 1)],
            pass_send.at[groups - 1, chunks - 1],
            pass_recv.at[groups - 1, chunks - 1],
            g,
        )

    def grad_copy(group, k):
        at = (pl.ds(group * GROUP, GROUP), columns(k))
        return remote(going.at[at], came.at[at], grad_send.at[group, k], grad_recv.at[group, k], f)

    def message(which, to):
        return remote(out_msg.at[which], in_msg.at[which], msg_send.at[which], msg_recv.at[which], to)

    def add_scores(at, k):
        s[at, :] += cross(x[at, columns(k)], x[0:both, columns(k)])

    def tile(block, group):
        return SCALE * s[part(block, group), :]

    def same_pair(group):
        row = lax.broadcasted_iota(jnp.int32, (GROUP, both), 0) + group * GROUP
        col = lax.broadcasted_iota(jnp.int32, (GROUP, both), 1)
        return (row == col) | (row == col + rows) | (row + rows == col), col < rows

    def column_lse(value):
        top = jnp.max(value, axis=0, keepdims=True)
        return top + jnp.log(jnp.sum(jnp.exp(value - top), axis=0, keepdims=True))

    def row_lse(value):
        top = jnp.max(value, axis=1, keepdims=True)
        return top + jnp.log(jnp.sum(jnp.exp(value - top), axis=1, keepdims=True))

    def post(which, row, to):
        out_msg[which] = jnp.broadcast_to(row, (8, rows))
        message(which, to).start()

    def weigh(block, group, column, across):
        value = across + jnp.exp(tile(block, group) - column)
        w[part(block, group), :] = value.astype(jnp.bfloat16)

    def turn(block):
        at = pl.ds(block * both, both)
        wt[:, at] = w[at, :].T

    def loop(body, steps=chunks):
        def step(k, _):
            body(k)
            return 0

        lax.fori_loop(0, steps, step, 0)

    barrier = pltpu.get_barrier_semaphore()
    for device in (p, r, f, g):
        pl.semaphore_signal(barrier, inc=1, device_id=(device,), device_id_type=MESH)
    s[...] = jnp.zeros_like(s)
    pl.semaphore_wait(barrier, 4)

    def send_first(k):
        far_copy(0, k).start()
        for half in range(2):
            own_copy(half, k).start()
            near_copy(half, k).start()

    loop(send_first)
    for group in range(1, groups - 1):
        loop(lambda k: far_copy(group, k).start())
    loop(lambda k: far_copy(groups - 1, k).start(), chunks - 1)
    direct_copy().start()
    far_copy(groups - 1, chunks - 1).start()

    def on_chip(k):
        for half in range(2):
            own_copy(half, k).wait()
            near_copy(half, k).wait_recv()
        add_scores(pl.ds(0, 2 * both), k)

    loop(on_chip)
    held = []
    for group in range(groups):
        same, query = same_pair(group)
        keep = query if group * GROUP >= rows else False
        held.append(column_lse(jnp.where(same & ~keep, -jnp.inf, tile(0, group))))
        held.append(column_lse(tile(1, group)))
    chip_lse = lse(*held)

    for group in range(groups):

        def off_chip(k):
            far_copy(group, k).wait_recv()
            pass_copy(group, k).start()
            add_scores(part(2, group), k)

            @pl.when(k > 0)
            def _():
                pass_copy(group, k - 1).wait_recv()
                add_scores(part(3, group), k - 1)

        last = group == groups - 1
        loop(off_chip, chunks - 1)
        if not last:
            far_copy(group, chunks - 1).wait_recv()
            pass_copy(group, chunks - 1).start()
            add_scores(part(2, group), chunks - 1)
        pass_copy(group, chunks - 2).wait_recv()
        add_scores(part(3, group), chunks - 2)
        pass_copy(group, chunks - 1).wait_recv()
        add_scores(part(3, group), chunks - 1)
        value = tile(3, group)
        stat[pl.ds(group * GROUP, GROUP), :] = jnp.broadcast_to(row_lse(value), (GROUP, 128))
        if last:
            theirs = as_row(lse(stat[0:rows, :], stat[rows:both, :]))
            post(0, theirs, f)
            chip_lse = lse(chip_lse, column_lse(value))
            far_copy(group, chunks - 1).wait_recv()
            add_scores(part(2, group), chunks - 1)
            chip_lse = lse(chip_lse, column_lse(tile(2, group)))
        else:
            chip_lse = lse(chip_lse, column_lse(value), column_lse(tile(2, group)))

    local = lse(chip_lse[:, :rows], chip_lse[:, rows:])
    post(1, local, g)
    message(0, f).wait_recv()
    norm = lse(local, in_msg[0, :1, :])
    norm_row = jnp.concatenate([norm, norm], axis=1)

    def across(block, group):
        return jnp.exp(tile(block, group) - norm_row)

    early = across(3, 0)
    message(1, g).wait_recv()
    far_norm = lse(in_msg[1, :1, :], theirs)

    for group in range(groups):
        first = group * GROUP % rows
        column = as_column(far_norm[:, first : first + GROUP])
        weigh(3, group, column, across(3, group) if group else early)

        def product(k):
            value = jnp.dot(w[part(3, group), :], x[0:both, columns(k)], preferred_element_type=jnp.float32)
            going[pl.ds(group * GROUP, GROUP), columns(k)] = (SCALE * value).astype(jnp.bfloat16)
            grad_copy(group, k).start()

        loop(product)
        if group == 0:
            post(2, norm, p)
            post(3, norm, r)
            norm_ref[...] = norm

    own_column = as_column(norm)
    for group in range(groups):
        same, query = same_pair(group)
        if group * GROUP >= rows:
            query = ~query
        first = group * GROUP % rows
        value = tile(0, group)
        one = across(0, group)
        value = one + jnp.exp(value - own_column[first : first + GROUP])
        value = jnp.where(same, jnp.where(query, 0.0, one - 1.0), value)
        wt[pl.ds(group * GROUP, GROUP), 0:both] = value.astype(jnp.bfloat16)
    for block, which, to in ((1, 2, p), (2, 3, r)):
        message(which, to).wait_recv()
        column = as_column(in_msg[which, :1, :])
        for group in range(groups):
            first = group * GROUP % rows
            weigh(block, group, column[first : first + GROUP], across(block, group))
    for block in (1, 2, 3):
        turn(block)

    def local_gradient(k):
        value = SCALE * jnp.dot(wt[...], x[:, columns(k)], preferred_element_type=jnp.float32)
        lq_ref[:, columns(k)] = value[:rows]
        ld_ref[:, columns(k)] = value[rows:]

    loop(local_gradient)

    def sent(k):
        for half in range(2):
            near_copy(half, k).wait_send()
        for group in range(groups):
            far_copy(group, k).wait_send()

    def passed(k):
        for group in range(groups - 1):
            pass_copy(group, k).wait_send()

    loop(sent)
    loop(passed)
    loop(lambda k: pass_copy(groups - 1, k).wait_send(), chunks - 1)
    direct_copy().wait_send()
    for which, to in enumerate((f, g, p, r)):
        message(which, to).wait_send()
    for group in range(groups):
        half, first = divmod(group * GROUP, rows)
        out = (lq_ref, ld_ref)[half]

        def add_terms(k):
            grad_copy(group, k).wait_recv()
            terms = came[pl.ds(group * GROUP, GROUP), columns(k)]
            out[pl.ds(first, GROUP), columns(k)] += terms.astype(jnp.float32)
            grad_copy(group, k).wait_send()

        loop(add_terms)


def write_out(norm_in, q_in, d_in, norm_out, q_out, d_out, sem):
    copies = []
    rows = q_in.shape[0] // PIECES
    for which, (source, target) in enumerate(((q_in, q_out), (d_in, d_out))):
        for piece in range(PIECES):
            at = pl.ds(piece * rows, rows)
            copies.append(pltpu.make_async_copy(source.at[at, :], target.at[at, :], sem.at[which, piece]))
    copies.append(pltpu.make_async_copy(norm_in, norm_out, sem.at[2, 0]))
    for copy in copies:
        copy.start()
    for copy in copies:
        copy.wait()


def on_device(queries, documents, count):
    rows, depth = queries.shape
    both = 2 * rows
    chunks = depth // WIDTH
    groups = both // GROUP
    dma = pltpu.SemaphoreType.DMA
    norm, grad_q, grad_d = pl.pallas_call(
        functools.partial(kernel, count),
        out_shape=(
            pltpu.VMEM((1, rows), jnp.float32),
            pltpu.VMEM((rows, depth), jnp.float32),
            pltpu.VMEM((rows, depth), jnp.float32),
        ),
        in_specs=[pl.BlockSpec(memory_space=pltpu.HBM)] * 2,
        out_specs=(pl.BlockSpec(memory_space=pltpu.VMEM),) * 3,
        scratch_shapes=[
            pltpu.VMEM((4 * both, depth), jnp.bfloat16),
            pltpu.VMEM((4 * both, both), jnp.float32),
            pltpu.VMEM((4 * both, both), jnp.bfloat16),
            pltpu.VMEM((both, 4 * both), jnp.bfloat16),
            pltpu.VMEM((both, depth), jnp.bfloat16),
            pltpu.VMEM((both, depth), jnp.bfloat16),
            pltpu.VMEM((both, 128), jnp.float32),
            pltpu.VMEM((4, 8, rows), jnp.float32),
            pltpu.VMEM((4, 8, rows), jnp.float32),
            dma((2, chunks)),
            dma((2, chunks)),
            dma((2, chunks)),
            dma((groups, chunks)),
            dma((groups, chunks)),
            dma((groups, chunks)),
            dma((groups, chunks)),
            dma((groups, chunks)),
            dma((groups, chunks)),
            dma((4,)),
            dma((4,)),
        ],
        compiler_params=pltpu.CompilerParams(
            collective_id=0, has_side_effects=True, vmem_limit_bytes=56 << 20
        ),
    )(queries, documents)
    norm, grad_q, grad_d = pl.pallas_call(
        write_out,
        out_shape=(
            jax.ShapeDtypeStruct((1, rows), jnp.float32),
            jax.ShapeDtypeStruct((rows, depth), jnp.float32),
            jax.ShapeDtypeStruct((rows, depth), jnp.float32),
        ),
        in_specs=[pl.BlockSpec(memory_space=pltpu.VMEM)] * 3,
        out_specs=(pl.BlockSpec(memory_space=pl.ANY),) * 3,
        scratch_shapes=[dma((3, PIECES))],
        compiler_params=pltpu.CompilerParams(vmem_limit_bytes=16 << 20),
    )(*[pltpu.with_memory_space_constraint(a, pltpu.VMEM) for a in (norm, grad_q, grad_d)])
    return norm.reshape(rows), grad_q, grad_d


def solution(mesh):
    return jax.shard_map(
        functools.partial(on_device, count=mesh.shape["dp"]),
        mesh=mesh,
        in_specs=(P("dp", None), P("dp", None)),
        out_specs=(P("dp"), P("dp", None), P("dp", None)),
        check_vma=False,
    )
```

```python
import functools

import jax
import jax.numpy as jnp
from jax import lax
from jax.experimental import pallas as pl
from jax.experimental.pallas import tpu as pltpu
from jax.sharding import PartitionSpec as P

MESH = pl.DeviceIdType.MESH
SCALE = 100.0
WIDTH = 512
GROUP = 128
PIECES = 4


def lse(*terms):
    highest = functools.reduce(jnp.maximum, terms)
    return highest + jnp.log(sum(jnp.exp(term - highest) for term in terms))


def as_column(row):
    return jnp.broadcast_to(row, (128, row.shape[1])).T[:, :1]


def as_row(column):
    return jnp.broadcast_to(column, (column.shape[0], 128)).T[:1, :]


def cross(left, right):
    return lax.dot_general(left, right, (((1,), (1,)), ((), ())), preferred_element_type=jnp.float32)


def kernel(
    count,
    q_ref,
    d_ref,
    norm_ref,
    lq_ref,
    ld_ref,
    x,
    s,
    w,
    wt,
    going,
    came,
    stat,
    out_msg,
    in_msg,
    own_sem,
    near_send,
    near_recv,
    far_send,
    far_recv,
    pass_send,
    pass_recv,
    grad_send,
    grad_recv,
    msg_send,
    msg_recv,
):
    rows, depth = q_ref.shape
    both = 2 * rows
    chunks = depth // WIDTH
    groups = both // GROUP
    me = lax.axis_index("dp")
    sign = 1 - 2 * lax.rem(me, 2)
    p = me + sign
    r = lax.rem(me - sign + count, count)
    f = lax.rem(me + 2 * sign + count, count)
    g = lax.rem(me - 2 * sign + count, count)

    def remote(src, dst, send, recv, to):
        return pltpu.make_async_remote_copy(
            src_ref=src, dst_ref=dst, send_sem=send, recv_sem=recv, device_id=(to,), device_id_type=MESH
        )

    def columns(k):
        return pl.ds(pl.multiple_of(k * WIDTH, WIDTH), WIDTH)

    def part(block, group):
        return pl.ds(block * both + group * GROUP, GROUP)

    def source(group):
        half, first = divmod(group * GROUP, rows)
        return (q_ref, d_ref)[half].at[pl.ds(first, GROUP), :]

    def own_copy(half, k):
        ref = (q_ref, d_ref)[half]
        return pltpu.make_async_copy(
            ref.at[:, columns(k)], x.at[pl.ds(half * rows, rows), columns(k)], own_sem.at[half, k]
        )

    def near_copy(half, k):
        ref = (q_ref, d_ref)[half]
        return remote(
            ref.at[:, columns(k)],
            x.at[pl.ds(both + half * rows, rows), columns(k)],
            near_send.at[half, k],
            near_recv.at[half, k],
            p,
        )

    def far_copy(group, k):
        return remote(
            source(group).at[:, columns(k)],
            x.at[part(2, group), columns(k)],
            far_send.at[group, k],
            far_recv.at[group, k],
            r,
        )

    def pass_copy(group, k):
        return remote(
            x.at[part(2, group), columns(k)],
            x.at[part(3, group), columns(k)],
            pass_send.at[group, k],
            pass_recv.at[group, k],
            p,
        )

    def direct_copy():
        return remote(
            source(groups - 1).at[:, columns(chunks - 1)],
            x.at[part(3, groups - 1), columns(chunks - 1)],
            pass_send.at[groups - 1, chunks - 1],
            pass_recv.at[groups - 1, chunks - 1],
            g,
        )

    def grad_copy(group, k):
        at = (pl.ds(group * GROUP, GROUP), columns(k))
        return remote(going.at[at], came.at[at], grad_send.at[group, k], grad_recv.at[group, k], f)

    def message(which, to):
        return remote(out_msg.at[which], in_msg.at[which], msg_send.at[which], msg_recv.at[which], to)

    def add_scores(at, k):
        s[at, :] += cross(x[at, columns(k)], x[0:both, columns(k)])

    def tile(block, group):
        return SCALE * s[part(block, group), :]

    def same_pair(group):
        row = lax.broadcasted_iota(jnp.int32, (GROUP, both), 0) + group * GROUP
        col = lax.broadcasted_iota(jnp.int32, (GROUP, both), 1)
        return (row == col) | (row == col + rows) | (row + rows == col), col < rows

    def column_lse(value):
        top = jnp.max(value, axis=0, keepdims=True)
        return top + jnp.log(jnp.sum(jnp.exp(value - top), axis=0, keepdims=True))

    def row_lse(value):
        top = jnp.max(value, axis=1, keepdims=True)
        return top + jnp.log(jnp.sum(jnp.exp(value - top), axis=1, keepdims=True))

    def post(which, row, to):
        out_msg[which] = jnp.broadcast_to(row, (8, rows))
        message(which, to).start()

    def weigh(block, group, column, row):
        first = group * GROUP % rows
        value = tile(block, group)
        value = jnp.exp(value - column[first : first + GROUP]) + jnp.exp(value - row)
        w[part(block, group), :] = value.astype(jnp.bfloat16)

    def turn(block):
        at = pl.ds(block * both, both)
        wt[:, at] = w[at, :].T

    def loop(body, steps=chunks):
        def step(k, _):
            body(k)
            return 0

        lax.fori_loop(0, steps, step, 0)

    barrier = pltpu.get_barrier_semaphore()
    for device in (p, r, f, g):
        pl.semaphore_signal(barrier, inc=1, device_id=(device,), device_id_type=MESH)

    def read_own(k):
        for half in range(2):
            own_copy(half, k).start()

    def send_near(k):
        for half in range(2):
            near_copy(half, k).start()

    loop(read_own)
    pl.semaphore_wait(barrier, 4)
    for group in range(groups - 1):
        loop(lambda k: far_copy(group, k).start())
    loop(lambda k: far_copy(groups - 1, k).start(), chunks - 1)
    direct_copy().start()
    far_copy(groups - 1, chunks - 1).start()
    loop(send_near)
    s[...] = jnp.zeros_like(s)

    def on_chip(k):
        for half in range(2):
            own_copy(half, k).wait()
            near_copy(half, k).wait_recv()
        add_scores(pl.ds(0, 2 * both), k)

    loop(on_chip)
    held = []
    for group in range(groups):
        same, query = same_pair(group)
        keep = query if group * GROUP >= rows else False
        held.append(column_lse(jnp.where(same & ~keep, -jnp.inf, tile(0, group))))
        held.append(column_lse(tile(1, group)))
    chip_lse = lse(*held)

    for group in range(groups):

        def off_chip(k):
            far_copy(group, k).wait_recv()
            pass_copy(group, k).start()
            add_scores(part(2, group), k)

            @pl.when(k > 0)
            def _():
                pass_copy(group, k - 1).wait_recv()
                add_scores(part(3, group), k - 1)

        last = group == groups - 1
        loop(off_chip, chunks - 1)
        if not last:
            far_copy(group, chunks - 1).wait_recv()
            pass_copy(group, chunks - 1).start()
            add_scores(part(2, group), chunks - 1)
        pass_copy(group, chunks - 2).wait_recv()
        add_scores(part(3, group), chunks - 2)
        pass_copy(group, chunks - 1).wait_recv()
        add_scores(part(3, group), chunks - 1)
        value = tile(3, group)
        stat[pl.ds(group * GROUP, GROUP), :] = jnp.broadcast_to(row_lse(value), (GROUP, 128))
        if last:
            theirs = as_row(lse(stat[0:rows, :], stat[rows:both, :]))
            post(0, theirs, f)
            chip_lse = lse(chip_lse, column_lse(value))
            far_copy(group, chunks - 1).wait_recv()
            add_scores(part(2, group), chunks - 1)
            chip_lse = lse(chip_lse, column_lse(tile(2, group)))
        else:
            chip_lse = lse(chip_lse, column_lse(value), column_lse(tile(2, group)))

    local = lse(chip_lse[:, :rows], chip_lse[:, rows:])
    post(1, local, g)
    message(0, f).wait_recv()
    norm = lse(local, in_msg[0, :1, :])
    norm_row = jnp.concatenate([norm, norm], axis=1)
    message(1, g).wait_recv()
    far_column = as_column(lse(in_msg[1, :1, :], theirs))

    for group in range(groups):
        weigh(3, group, far_column, norm_row)

        def product(k):
            value = jnp.dot(w[part(3, group), :], x[0:both, columns(k)], preferred_element_type=jnp.float32)
            going[pl.ds(group * GROUP, GROUP), columns(k)] = (SCALE * value).astype(jnp.bfloat16)
            grad_copy(group, k).start()

        loop(product)
        if group == 0:
            post(2, norm, p)
            post(3, norm, r)
            norm_ref[...] = norm

    own_column = as_column(norm)
    for group in range(groups):
        same, query = same_pair(group)
        if group * GROUP >= rows:
            query = ~query
        first = group * GROUP % rows
        value = tile(0, group)
        across = jnp.exp(value - norm_row)
        value = across + jnp.exp(value - own_column[first : first + GROUP])
        value = jnp.where(same, jnp.where(query, 0.0, across - 1.0), value)
        wt[pl.ds(group * GROUP, GROUP), 0:both] = value.astype(jnp.bfloat16)
    for block, which, to in ((1, 2, p), (2, 3, r)):
        message(which, to).wait_recv()
        column = as_column(in_msg[which, :1, :])
        for group in range(groups):
            weigh(block, group, column, norm_row)
    for block in (1, 2, 3):
        turn(block)

    def local_gradient(k):
        value = SCALE * jnp.dot(wt[...], x[:, columns(k)], preferred_element_type=jnp.float32)
        lq_ref[:, columns(k)] = value[:rows]
        ld_ref[:, columns(k)] = value[rows:]

    loop(local_gradient)

    def sent(k):
        for half in range(2):
            near_copy(half, k).wait_send()
        for group in range(groups):
            far_copy(group, k).wait_send()

    def passed(k):
        for group in range(groups - 1):
            pass_copy(group, k).wait_send()

    loop(sent)
    loop(passed)
    loop(lambda k: pass_copy(groups - 1, k).wait_send(), chunks - 1)
    direct_copy().wait_send()
    for which, to in enumerate((f, g, p, r)):
        message(which, to).wait_send()
    for group in range(groups):
        half, first = divmod(group * GROUP, rows)
        out = (lq_ref, ld_ref)[half]

        def add_terms(k):
            grad_copy(group, k).wait_recv()
            terms = came[pl.ds(group * GROUP, GROUP), columns(k)]
            out[pl.ds(first, GROUP), columns(k)] += terms.astype(jnp.float32)
            grad_copy(group, k).wait_send()

        loop(add_terms)


def write_out(norm_in, q_in, d_in, norm_out, q_out, d_out, sem):
    copies = []
    rows = q_in.shape[0] // PIECES
    for which, (source, target) in enumerate(((q_in, q_out), (d_in, d_out))):
        for piece in range(PIECES):
            at = pl.ds(piece * rows, rows)
            copies.append(pltpu.make_async_copy(source.at[at, :], target.at[at, :], sem.at[which, piece]))
    copies.append(pltpu.make_async_copy(norm_in, norm_out, sem.at[2, 0]))
    for copy in copies:
        copy.start()
    for copy in copies:
        copy.wait()


def on_device(queries, documents, count):
    rows, depth = queries.shape
    both = 2 * rows
    chunks = depth // WIDTH
    groups = both // GROUP
    dma = pltpu.SemaphoreType.DMA
    norm, grad_q, grad_d = pl.pallas_call(
        functools.partial(kernel, count),
        out_shape=(
            pltpu.VMEM((1, rows), jnp.float32),
            pltpu.VMEM((rows, depth), jnp.float32),
            pltpu.VMEM((rows, depth), jnp.float32),
        ),
        in_specs=[pl.BlockSpec(memory_space=pltpu.HBM)] * 2,
        out_specs=(pl.BlockSpec(memory_space=pltpu.VMEM),) * 3,
        scratch_shapes=[
            pltpu.VMEM((4 * both, depth), jnp.bfloat16),
            pltpu.VMEM((4 * both, both), jnp.float32),
            pltpu.VMEM((4 * both, both), jnp.bfloat16),
            pltpu.VMEM((both, 4 * both), jnp.bfloat16),
            pltpu.VMEM((both, depth), jnp.bfloat16),
            pltpu.VMEM((both, depth), jnp.bfloat16),
            pltpu.VMEM((both, 128), jnp.float32),
            pltpu.VMEM((4, 8, rows), jnp.float32),
            pltpu.VMEM((4, 8, rows), jnp.float32),
            dma((2, chunks)),
            dma((2, chunks)),
            dma((2, chunks)),
            dma((groups, chunks)),
            dma((groups, chunks)),
            dma((groups, chunks)),
            dma((groups, chunks)),
            dma((groups, chunks)),
            dma((groups, chunks)),
            dma((4,)),
            dma((4,)),
        ],
        compiler_params=pltpu.CompilerParams(
            collective_id=0, has_side_effects=True, vmem_limit_bytes=56 << 20
        ),
    )(queries, documents)
    norm, grad_q, grad_d = pl.pallas_call(
        write_out,
        out_shape=(
            jax.ShapeDtypeStruct((1, rows), jnp.float32),
            jax.ShapeDtypeStruct((rows, depth), jnp.float32),
            jax.ShapeDtypeStruct((rows, depth), jnp.float32),
        ),
        in_specs=[pl.BlockSpec(memory_space=pltpu.VMEM)] * 3,
        out_specs=(pl.BlockSpec(memory_space=pl.ANY),) * 3,
        scratch_shapes=[dma((3, PIECES))],
        compiler_params=pltpu.CompilerParams(vmem_limit_bytes=16 << 20),
    )(*[pltpu.with_memory_space_constraint(a, pltpu.VMEM) for a in (norm, grad_q, grad_d)])
    return norm.reshape(rows), grad_q, grad_d


def solution(mesh):
    return jax.shard_map(
        functools.partial(on_device, count=mesh.shape["dp"]),
        mesh=mesh,
        in_specs=(P("dp", None), P("dp", None)),
        out_specs=(P("dp"), P("dp", None), P("dp", None)),
        check_vma=False,
    )
```
